32 devices in a mesh: row: 4 (over z), col: 8 (over y, x, core).
Axes of the slice: x: 2, y: 2, z: 4, core: 2. Of those that a mesh axis runs over, the one named last changes fastest.
Arguments:
- factor: bfloat16 [16384, 16384], P('row', 'col'), may hold values from -1 to 7, as said below
- old_basis: bfloat16 [16384, 2048], P(('col', 'row')), may hold values from -9 to 9, as said below
- first_moment: float32 [16384, 2048], P(('col', 'row')), may hold values from -1.8 to 1.8
Outputs:
- new_basis: bfloat16 [16384, 2048], P(('col', 'row'))
- rotated_moment: float32 [16384, 2048], P(('col', 'row'))
The draws below stay inside these ranges and needn't reach their ends.
Inputs may be any that keep to these rules, and one draw needn't show every extreme that they name: factor equals its transpose and is positive definite. old_basis has full column rank.
All inputs are finite; a program needn't handle non-finite values.
Results may differ from the reference program's by a relative error of at most 0.0053.
Values may be sent and summed in bfloat16 or wider, within the bound.
No kernel may reach another device: no remote copies, remote signals or barrier semaphores. Data moves between devices by JAX's collectives and lax.ppermute only.
A program may use at most 192 MiB of HBM per device.

```python
import math
import jax
import jax.numpy as jnp
from jax import lax

M = 16384
K = 2048


def draw_factor(key, part):
    key = jax.random.fold_in(key, 11)
    noise_key, diag_key = jax.random.split(key)
    noise = jnp.clip(jax.random.normal(noise_key, (M, M), jnp.float32), -5.0, 5.0)
    spread = (noise + noise.T) * (0.6 / math.sqrt(2.0 * M))
    diagonal = jnp.exp(jax.random.uniform(diag_key, (M,), jnp.float32, math.log(2.0), math.log(6.0)))
    places = jnp.arange(M)
    spread = spread.at[places, places].add(diagonal)
    return spread.astype(jnp.bfloat16)


def draw_old_basis(key, part):
    key = jax.random.fold_in(key, 23)
    values = jnp.clip(jax.random.normal(key, (M, K), jnp.float32), -4.5, 4.5)
    ramp = 0.6 + 1.2 * (jnp.arange(M, dtype=jnp.float32) + 0.5) / M
    return (values * ramp[:, None]).astype(jnp.bfloat16)


def block_levels(key, extent, cuts, least, high):
    level = 1.0
    for axis_at, shards_of in cuts:
        heights = jax.random.uniform(jax.random.fold_in(jax.random.fold_in(key, 6), axis_at), (shards_of,), jnp.float32, least / len(cuts), high / len(cuts))
        level = level * jnp.repeat(jnp.exp(heights), extent[axis_at] // shards_of).reshape((-1,) + (1,) * (len(extent) - 1 - axis_at))
    return level


def centred(stream_key, extent, deviation, most, cuts=(), kind=jnp.bfloat16):
    loudness = block_levels(stream_key, extent, cuts, -0.22, 0.18) if cuts else 1.0
    values = jax.random.normal(stream_key, extent, jnp.float32) * deviation * loudness
    return jnp.minimum(jnp.maximum(values, -most), most).astype(kind)


def setup_inputs(seed: int = 0) -> dict:
    arg_keys = jax.random.split(jax.random.key(seed), 4)
    factor = draw_factor(jax.random.fold_in(arg_keys[3], 71), 0)
    old_basis = draw_old_basis(jax.random.fold_in(arg_keys[3], 71), 0)
    first_moment = centred(arg_keys[2], (M, K), 0.3, 1.8, ((0, 32),), jnp.float32)
    return dict(factor=factor, old_basis=old_basis, first_moment=first_moment)


def reference(factor, old_basis, first_moment):
    block_rows = M // 8
    blocks = factor.reshape(8, block_rows, M)

    def one_block(row_block):
        return jnp.dot(row_block.astype(jnp.float32), old_basis.astype(jnp.float32), preferred_element_type=jnp.float32).astype(jnp.bfloat16)
    product = lax.map(one_block, blocks).reshape(M, K)
    gram_matrix = lax.dot_general(product.astype(jnp.float32), product.astype(jnp.float32), (((0,), (0,)), ((), ())), preferred_element_type=jnp.float32)
    gram_matrix = gram_matrix * (1.0 / M)
    lower_factor = jnp.linalg.cholesky(gram_matrix)
    solved = jax.scipy.linalg.solve_triangular(lower_factor, product.astype(jnp.float32).T, lower=True)
    new_basis = solved.T.astype(jnp.bfloat16)
    rotated_moment = jnp.dot(first_moment, lower_factor, precision=lax.Precision.HIGHEST)
    return (new_basis, rotated_moment)
```

```python
import functools

import jax
import jax.numpy as jnp
from jax import lax
from jax.experimental import pallas as pl
from jax.experimental.pallas import tpu as pltpu
from jax.sharding import PartitionSpec as P

F32 = jnp.float32
BF16 = jnp.bfloat16
LEAF = 128
GROUP = 8
STRIP = 4 * LEAF


def pieces(values):
    high = values.astype(BF16)
    rest = values - high.astype(F32)
    middle = rest.astype(BF16)
    low = (rest - middle.astype(F32)).astype(BF16)
    return high, middle, low


def left_form(values):
    high, middle, low = pieces(values)
    return jnp.concatenate([high, high, middle, high, low, middle], 1)


def right_form(values):
    high, middle, low = pieces(values)
    return jnp.concatenate([high, middle, high, low, high, middle], 1)


def times_transposed(left, right):
    return lax.dot_general(left, right, (((1,), (1,)), ((), ())), preferred_element_type=F32)


def full_times_transposed(left, right):
    return times_transposed(left_form(left), right_form(right))


def leaf_factor(block):
    size = block.shape[0]
    groups = size // GROUP
    shape = (GROUP, size)
    lane = lax.broadcasted_iota(jnp.int32, shape, 1)
    sub = lax.broadcasted_iota(jnp.int32, shape, 0)
    rows = [block[GROUP * g : GROUP * (g + 1), :] for g in range(groups)]
    upper, inverse = [], []
    for g in range(groups):
        first = GROUP * g
        inside = (lane >= first) & (lane < first + GROUP)
        columns = {
            h: [
                jnp.broadcast_to(rows[h][:, first + c : first + c + 1], shape)
                for c in range(GROUP)
            ]
            for h in range(g, groups)
        }
        rows[g] = jnp.where(inside, jnp.where(lane == sub + first, 1.0, 0.0), rows[g])
        for h in range(g + 1, groups):
            rows[h] = jnp.where(inside, 0.0, rows[h])
        scale = jnp.ones(shape, F32)
        for c in range(GROUP):
            pivot = jnp.broadcast_to(columns[g][c][c : c + 1, :], shape)
            root = lax.rsqrt(pivot)
            ratio = root * root
            scale = jnp.where(sub == c, root, scale)
            factors = {g: jnp.where(sub > c, columns[g][c] * ratio, 0.0)}
            for h in range(g + 1, groups):
                factors[h] = columns[h][c] * ratio
            for later in range(c + 1, GROUP):
                entry = jnp.broadcast_to(columns[g][later][c : c + 1, :], shape)
                for h in range(g, groups):
                    columns[h][later] = columns[h][later] - factors[h] * entry
            pivot_row = jnp.broadcast_to(rows[g][c : c + 1, :], shape)
            for h in range(g, groups):
                rows[h] = rows[h] - factors[h] * pivot_row
        top = rows[g]
        for c in range(GROUP):
            top = jnp.where(lane == first + c, columns[g][c], top)
        upper.append(jnp.where(lane >= sub + first, top * scale, 0.0))
        inverse.append(jnp.where(lane <= sub + first, rows[g] * scale, 0.0))
    return jnp.concatenate(upper, 0).T, jnp.concatenate(inverse, 0)


def panel_kernel(strip, groups, *refs):
    gram_refs = refs[: len(groups)]
    product_ref, moment_ref, basis_ref, rotated_ref = refs[len(groups) : len(groups) + 4]
    work, rest, left_panel, right_panel, arrivals = refs[len(groups) + 4 :]
    width = work.shape[0]
    strips = width // strip
    double = 2 * LEAF

    copies = []
    for group, gram_ref in zip(groups, gram_refs):
        begin = 0
        for s in group:
            length = (s + 1) * strip
            copies.append(
                pltpu.make_async_copy(
                    gram_ref.at[:, pl.ds(begin, length)],
                    work.at[pl.ds(s * strip, strip), pl.ds(0, length)],
                    arrivals.at[s],
                )
            )
            begin += length
    for copy in copies:
        copy.start()
    rest[...] = product_ref[...].astype(F32)
    for copy in copies:
        copy.wait()

    row_ids = lax.broadcasted_iota(jnp.int32, (strip, double), 0)

    def step(k, carry):
        here = pl.multiple_of(k * double, double)
        half = pl.multiple_of(here + LEAF, LEAF)
        below = here + double
        factor_a, inverse_a = leaf_factor(work[pl.ds(here, LEAF), pl.ds(here, LEAF)])
        side = full_times_transposed(work[pl.ds(half, LEAF), pl.ds(here, LEAF)], inverse_a)
        corner = work[pl.ds(half, LEAF), pl.ds(half, LEAF)] - full_times_transposed(side, side)
        factor_b, inverse_b = leaf_factor(corner)
        cross = full_times_transposed(side, inverse_a.T)
        inverse_side = -full_times_transposed(inverse_b, cross.T)
        work[pl.ds(here, LEAF), pl.ds(here, LEAF)] = factor_a
        work[pl.ds(half, LEAF), pl.ds(here, LEAF)] = side
        work[pl.ds(half, LEAF), pl.ds(half, LEAF)] = factor_b
        nothing = jnp.zeros((LEAF, LEAF), F32)
        inverse = jnp.concatenate(
            [
                jnp.concatenate([inverse_a, nothing], 1),
                jnp.concatenate([inverse_side, inverse_b], 1),
            ],
            0,
        )
        inverse_form = right_form(inverse)

        solved = times_transposed(left_form(rest[:, pl.ds(here, double)]), inverse_form)
        basis_ref[:, pl.ds(here, double)] = solved.astype(BF16)
        solved_form = left_form(solved)

        first_tile = below // strip

        def one_panel(tile, carry):
            at = pl.multiple_of(tile * strip, strip)
            old = work[pl.ds(at, strip), pl.ds(here, double)]
            new = times_transposed(left_form(old), inverse_form)
            live = row_ids + at >= below
            work[pl.ds(at, strip), pl.ds(here, double)] = jnp.where(live, new, old)
            new = jnp.where(live, new, 0.0)
            left_panel[pl.ds(at, strip), :] = left_form(new)
            right_panel[pl.ds(at, strip), :] = right_form(new)
            return carry

        lax.fori_loop(first_tile, strips, one_panel, 0)

        def one_strip(column, carry):
            at = pl.multiple_of(column * strip, strip)
            right = right_panel[pl.ds(at, strip), :]
            rest[:, pl.ds(at, strip)] -= times_transposed(solved_form, right)

            def one_tile(tile, carry):
                top = pl.multiple_of(tile * strip, strip)
                work[pl.ds(top, strip), pl.ds(at, strip)] -= times_transposed(
                    left_panel[pl.ds(top, strip), :], right_panel[pl.ds(at, strip), :]
                )
                return carry

            return lax.fori_loop(column, strips, one_tile, carry)

        lax.fori_loop(first_tile, strips, one_strip, 0)
        return carry

    lax.fori_loop(0, width // double, step, 0)

    tile_rows = lax.broadcasted_iota(jnp.int32, (strip, strip), 0)
    tile_columns = lax.broadcasted_iota(jnp.int32, (strip, strip), 1)

    def rotate_strip(column, carry):
        at = pl.multiple_of(column * strip, strip)
        rotated_ref[:, pl.ds(at, strip)] = jnp.zeros((rotated_ref.shape[0], strip), F32)

        def rotate_tile(tile, carry):
            top = pl.multiple_of(tile * strip, strip)
            lower = work[pl.ds(top, strip), pl.ds(at, strip)]
            lower = jnp.where(tile_rows + top >= tile_columns + at, lower, 0.0)
            lower_high = lower.astype(BF16)
            lower_rest = (lower - lower_high.astype(F32)).astype(BF16)
            moment = moment_ref[:, pl.ds(top, strip)]
            moment_high = moment.astype(BF16)
            moment_rest = (moment - moment_high.astype(F32)).astype(BF16)
            rotated_ref[:, pl.ds(at, strip)] += jnp.dot(
                jnp.concatenate([moment_high, moment_high, moment_rest], 1),
                jnp.concatenate([lower_high, lower_rest, lower_high], 0),
                preferred_element_type=F32,
            )
            return carry

        return lax.fori_loop(column, strips, rotate_tile, carry)

    lax.fori_loop(0, strips, rotate_strip, 0)


def factor_and_apply(gram_groups, groups, product, moment, strip):
    slab, width = product.shape
    return pl.pallas_call(
        functools.partial(panel_kernel, strip, groups),
        out_shape=(
            jax.ShapeDtypeStruct((slab, width), BF16),
            jax.ShapeDtypeStruct((slab, width), F32),
        ),
        in_specs=[
            *[pl.BlockSpec(memory_space=pl.ANY) for _ in groups],
            pl.BlockSpec(memory_space=pltpu.VMEM),
            pl.BlockSpec(memory_space=pltpu.VMEM),
        ],
        out_specs=(
            pl.BlockSpec(memory_space=pltpu.VMEM),
            pl.BlockSpec(memory_space=pltpu.VMEM),
        ),
        scratch_shapes=[
            pltpu.VMEM((width, width), F32),
            pltpu.VMEM((slab, width), F32),
            pltpu.VMEM((width, 12 * LEAF), BF16),
            pltpu.VMEM((width, 12 * LEAF), BF16),
            pltpu.SemaphoreType.DMA((width // strip,)),
        ],
        compiler_params=pltpu.CompilerParams(vmem_limit_bytes=60 * 2**20),
        cost_estimate=pl.CostEstimate(
            flops=40 * 10**9, bytes_accessed=24 * 2**20, transcendentals=0
        ),
    )(*gram_groups, product, moment)


def bits_of(axis):
    size = lax.axis_size(axis)
    return [(axis, 1 << place) for place in range(size.bit_length() - 1)]


def side_of(dim):
    axis, bit = dim
    return (lax.axis_index(axis) // bit) % 2


def swap(values, dim):
    axis, bit = dim
    return lax.ppermute(values, axis, [(i, i ^ bit) for i in range(lax.axis_size(axis))])


def halve(values, dim, at):
    side = side_of(dim)
    size = values.shape[at] // 2
    kept = lax.dynamic_slice_in_dim(values, side * size, size, at)
    sent = lax.dynamic_slice_in_dim(values, (1 - side) * size, size, at)
    return kept + swap(sent, dim)


def double(values, dim):
    first = side_of(dim) == 0
    other = swap(values, dim)
    return jnp.concatenate([jnp.where(first, values, other), jnp.where(first, other, values)], 0)


def gather_rows(block):
    size = lax.axis_size("row")
    me = lax.axis_index("row")
    rows = block.shape[0]
    upward, downward = [block], [block]
    for step in range(1, size):
        upward.append(
            lax.ppermute(upward[-1], "row", [(i, i + 1) for i in range(step - 1, size - 1)])
        )
        downward.append(
            lax.ppermute(downward[-1], "row", [(i + 1, i) for i in range(size - step)])
        )
    panel = jnp.zeros((size * rows, block.shape[1]), block.dtype)
    for step in range(size):
        held = block
        if step > 0:
            held = jnp.where(me >= step, upward[step], downward[size - step])
        source = lax.rem(me - step + size, size)
        panel = lax.dynamic_update_slice_in_dim(panel, held, source * rows, 0)
    return panel


def scatter_columns(partial, slab_rows):
    dims = bits_of("col")
    count = len(dims)
    width = partial.shape[1]
    blocks = partial.reshape((2,) * count + (slab_rows, width))
    blocks = halve(blocks, dims[0], count - 1)
    blocks = blocks.reshape((2,) * (count - 1) + (slab_rows, width))
    others = dims[1:]
    finished = []
    for turn in range(2):
        piece = blocks[..., turn * (width // 2) : (turn + 1) * (width // 2)]
        order = list(range(count - 1))
        if turn == 1:
            order.reverse()
        for which in order:
            piece = halve(piece, others[which], count - 2 - which)
        finished.append(piece.reshape(slab_rows, width // 2))
    return jnp.concatenate(finished, 1)


def sum_gram(half, core, others):
    rows = half.shape[0] // 2
    finished = []
    for turn in range(2):
        piece = half[turn * rows : (turn + 1) * rows]
        order = list(others)
        if turn == 1:
            order[0], order[1] = order[1], order[0]
        for dim in order:
            piece = halve(piece, dim, 0)
        for dim in reversed(order):
            piece = double(piece, dim)
        finished.append(piece)
    return double(jnp.concatenate(finished, 0), core)


def body(factor, old_basis, first_moment):
    grid_rows = lax.axis_size("row")
    grid_columns = lax.axis_size("col")
    slab_rows, panel_width = old_basis.shape
    total_rows = slab_rows * grid_rows * grid_columns
    count = panel_width // STRIP
    core, *others = bits_of("col")
    others = others + bits_of("row")
    core_side = side_of(core)
    to_owner = [
        (slab, (slab % grid_rows) * grid_columns + slab // grid_rows)
        for slab in range(grid_rows * grid_columns)
    ]
    groups = [tuple(range(count - 2))] if count > 2 else []
    groups += [(s,) for s in range(max(count - 2, 0), count)]

    shared, owned, gram_groups = [], [], []
    for chunk in range(count):
        panel = gather_rows(old_basis[:, chunk * STRIP : (chunk + 1) * STRIP])
        partial = jnp.dot(factor, panel, preferred_element_type=F32)
        landed = scatter_columns(partial, slab_rows).astype(BF16)
        shared.append(jnp.concatenate([landed, swap(landed, core)], 0))
        owned.append(lax.ppermute(landed, ("row", "col"), to_owner))
        for group in groups:
            if group[-1] != chunk:
                continue
            parts = []
            for s in group:
                mine = lax.dynamic_slice_in_dim(
                    shared[s], core_side * (STRIP // 2), STRIP // 2, 1
                )
                for t in range(s + 1):
                    parts.append(
                        lax.dot_general(
                            mine, shared[t], (((0,), (0,)), ((), ())),
                            preferred_element_type=F32,
                        )
                    )
            half = jnp.concatenate(parts, 1) * (1.0 / total_rows)
            gram_groups.append(sum_gram(half, core, others))
    product = jnp.concatenate(owned, 1)
    return factor_and_apply(gram_groups, groups, product, first_moment, STRIP)


def solution(mesh):
    placed = (P("row", "col"), P(("col", "row"), None), P(("col", "row"), None))
    return jax.shard_map(
        body,
        mesh=mesh,
        in_specs=placed,
        out_specs=(P(("col", "row"), None), P(("col", "row"), None)),
        check_vma=False,
    )
```
